128 devices in a mesh: row: 8 (over y_lo, z), col: 16 (over x, y_hi, core).
Axes of the slice: x: 4, y: 4 (y_hi: 2, y_lo: 2; y = y_hi * 2 + y_lo), z: 4, core: 2. Of those that a mesh axis runs over, the one named last changes fastest.
Arguments:
- inputs: bfloat16 [1024, 8192], P('col', 'row'), may hold values from -6 to 6
- cotangent: bfloat16 [1024, 8192], P('col', 'row'), may hold values from -6 to 6
- gate_weight: bfloat16 [8192, 14336], P('row', 'col'), may hold values from -0.0625 to 0.0625
- up_weight: bfloat16 [8192, 14336], P('row', 'col'), may hold values from -0.0625 to 0.0625
- down_weight: bfloat16 [14336, 8192], P('col', 'row'), may hold values from -0.046875 to 0.046875
Outputs:
- input_grad: bfloat16 [1024, 8192], P('col', 'row')
- gate_grad: bfloat16 [8192, 14336], P('row', 'col')
- up_grad: bfloat16 [8192, 14336], P('row', 'col')
- down_grad: bfloat16 [14336, 8192], P('col', 'row')
The draws below stay inside these ranges and needn't reach their ends.
All inputs are finite; a program needn't handle non-finite values.
Results may differ from the reference program's by a relative error of at most 0.005.
Values may be sent and summed in bfloat16 or wider, within the bound.
A program may use at most 128 MiB of HBM per device.

```python
import jax
import jax.numpy as jnp

D = 8192
FF = 14336
TOKENS = 1024


def levels(key, shape, pieces, least, largest):
    def one(axis_at, parts):
        heights = jax.random.uniform(jax.random.fold_in(jax.random.fold_in(key, 6), axis_at), (parts,), jnp.float32, least / len(pieces), largest / len(pieces))
        return jnp.repeat(jnp.exp(heights), shape[axis_at] // parts).reshape((-1,) + (1,) * (len(shape) - axis_at - 1))

    gain = one(*pieces[0])
    for cut in pieces[1:]:
        gain = gain * one(*cut)
    return gain


def noise(stream_key, shape, width, bound, cuts=(), kind=jnp.bfloat16):
    result = width * jax.random.normal(stream_key, shape, jnp.float32)
    if cuts:
        result = result * levels(stream_key, shape, cuts, -0.22, 0.18)
    return jnp.clip(result, -bound, bound).astype(kind)


def setup_inputs(seed: int = 0) -> dict:
    seeds = jax.random.split(jax.random.key(seed), 6)
    return {
        "inputs": noise(seeds[0], (TOKENS, D), 1.0, 6.0, ((0, 16), (1, 8))),
        "cotangent": noise(seeds[1], (TOKENS, D), 1.0, 6.0, ((0, 16), (1, 8))),
        "gate_weight": noise(seeds[2], (D, FF), D ** -0.5, 0.0625, ((0, 8), (1, 16))),
        "up_weight": noise(seeds[3], (D, FF), D ** -0.5, 0.0625, ((0, 8), (1, 16))),
        "down_weight": noise(seeds[4], (FF, D), FF ** -0.5, 0.046875, ((0, 16), (1, 8))),
    }


def reference(inputs, cotangent, gate_weight, up_weight, down_weight):
    gate = jnp.dot(inputs, gate_weight, preferred_element_type=jnp.float32)
    up = jnp.dot(inputs, up_weight, preferred_element_type=jnp.float32)
    sig = jax.nn.sigmoid(gate)
    act = gate * sig
    deriv = sig * (1.0 + gate * (1.0 - sig))
    hidden = (act * up).astype(jnp.bfloat16)
    slope = jnp.dot(cotangent, down_weight.T, preferred_element_type=jnp.float32)
    gate_delta = (slope * up * deriv).astype(jnp.bfloat16)
    up_delta = (slope * act).astype(jnp.bfloat16)
    down_grad = jnp.dot(hidden.T, cotangent, preferred_element_type=jnp.float32).astype(jnp.bfloat16)
    gate_grad = jnp.dot(inputs.T, gate_delta, preferred_element_type=jnp.float32).astype(jnp.bfloat16)
    up_grad = jnp.dot(inputs.T, up_delta, preferred_element_type=jnp.float32).astype(jnp.bfloat16)
    input_grad = jnp.dot(gate_delta, gate_weight.T, preferred_element_type=jnp.float32)
    input_grad = input_grad + jnp.dot(up_delta, up_weight.T, preferred_element_type=jnp.float32)
    return input_grad.astype(jnp.bfloat16), gate_grad, up_grad, down_grad
```

```python
import jax
import jax.numpy as jnp
from jax import lax
from jax.experimental import pallas as pl
from jax.experimental.pallas import tpu as pltpu
from jax.sharding import PartitionSpec as P

MESH = pl.DeviceIdType.MESH
F32, BF16 = jnp.float32, jnp.bfloat16
NB = 4
NZ, NY, NX, NH, NC = 4, 2, 4, 2, 2

ORDER = (
    "a1:0", "a2:0", "a1:1", "a2:1", "a1:2", "a3:0", "w:0", "s1:0", "a3:1", "s2:0", "a2:2", "s1:1", "s2:1",
    "a3:2", "s4:0", "a1:3", "s3:0", "s4:1", "s3:1", "s5:0", "s1:2", "a2:3", "s6a:0", "a3:3", "s5:1", "s1:3",
    "s2:2", "s2:3", "s6a:1", "s6b:0", "s4:2", "s4:3", "s6c:0", "s3:2", "s6c:1", "s3:3", "s5:2", "s7:0",
    "s8:0", "s6b:1", "s10:0", "s6a:2", "s5:3", "s8:1", "s6a:3", "s7:1", "s10:1", "s6c:2", "s6b:2", "s11:0",
    "s11:1", "s6c:3", "s6b:3", "s8:2", "s9:0", "s7:2", "s10:2", "s8:3", "s12:1", "s7:3", "s10:3", "s9:1",
    "s11:2", "s9:2", "g:0", "s11:3", "s9:3", "s12:0", "g:2", "g:3", "g:1", "s12:2", "s12:3",
)


def nn(a, b):
    return lax.dot_general(a, b, (((1,), (0,)), ((), ())), preferred_element_type=F32)


def nt(a, b):
    return lax.dot_general(a, b, (((1,), (1,)), ((), ())), preferred_element_type=F32)


def tn(a, b):
    return lax.dot_general(a, b, (((0,), (0,)), ((), ())), preferred_element_type=F32)


def scratch(dims):
    D, F, T, R, O = dims["D"], dims["F"], dims["T"], dims["R"], dims["O"]
    v = pltpu.VMEM
    return {
        "wg": v((D, F), BF16),
        "wu": v((D, F), BF16),
        "wd": v((F, D), BF16),
        "xa": v((2, NB, NX * NH, NC, R, D), BF16),
        "part": v((2, 3, NZ, NY, O, F), F32),
        "far_s": v((NB, 2, 2, O, F), BF16),
        "far_r": v((NB, 2, 2, O, F), BF16),
        "dir_s": v((NB, 2, 2, O, F), BF16),
        "dir_r": v((NB, 2, 2, O, F), BF16),
        "rel_s": v((NB, 2, 2, O, F), BF16),
        "rel_r": v((NB, 2, 2, O, F), BF16),
        "zsum": v((NB, NY, 2, O, F), F32),
        "gy_r": v((NB, 2, O, F), F32),
        "sy_s": v((NB, NZ, O, F), BF16),
        "sy_r": v((NB, NZ, O, F), BF16),
        "sz_s": v((NB, 3, O, F), BF16),
        "sz_r": v((NB, 3, O, F), BF16),
        "s_own": v((NB, O, F), F32),
        "hgu": v((3, NB, NZ, NY, O, F), BF16),
        "igp": v((NB, NX * NH, NC, R, D), F32),
        "co_r": v((NB, NX * NH, R, D), F32),
        "xs_s": v((NB, 3, NH, R, D), BF16),
        "xs_r": v((NB, 3, NH, R, D), BF16),
        "igx": v((NB, NH, R, D), F32),
        "h_r": v((NB, R, D), F32),
        "acc_g": v((D, F), F32),
        "acc_u": v((D, F), F32),
        "acc_d": v((F, D), F32),
        "st_g": v((D, F), BF16),
        "st_u": v((D, F), BF16),
        "st_d": v((F, D), BF16),
        "ssem": pltpu.SemaphoreType.DMA((NB * 40,)),
        "rsem": pltpu.SemaphoreType.DMA((NB * 40,)),
        "lsem": pltpu.SemaphoreType.DMA((8,)),
    }


def kernel(dims, names, x_ref, c_ref, wg_hbm, wu_hbm, wd_hbm, ig_ref, gg_hbm, ug_hbm, dg_hbm, *refs):
    D, F, T, R, O = dims["D"], dims["F"], dims["T"], dims["R"], dims["O"]
    s = dict(zip(names, refs))
    row, col = lax.axis_index("row"), lax.axis_index("col")
    yi, zi = row // NZ, row % NZ
    xi, hi, ci = col // (NH * NC), (col // NC) % NH, col % NC
    y_o, h_o, c_o = 1 - yi, 1 - hi, 1 - ci

    def zn(k):
        return (zi + k) % NZ

    def xn(k):
        return (xi + k) % NX

    def at_z(k):
        return (yi * NZ + zn(k), col)

    def at_x(k):
        return (row, xn(k) * (NH * NC) + hi * NC + ci)

    at_y = (y_o * NZ + zi, col)
    at_h = (row, xi * (NH * NC) + h_o * NC + ci)
    at_c = (row, xi * (NH * NC) + hi * NC + c_o)

    loads = [
        pltpu.make_async_copy(src, s[dst], s["lsem"].at[i])
        for i, (src, dst) in enumerate(((wg_hbm, "wg"), (wu_hbm, "wu"), (wd_hbm, "wd")))
    ]
    for load in loads:
        load.start()

    barrier = pltpu.get_barrier_semaphore()
    peers = [at_z(1), at_z(2), at_z(3), at_x(1), at_x(2), at_x(3), at_y, at_h, at_c]
    for peer in peers:
        pl.semaphore_signal(barrier, inc=1, device_id=peer, device_id_type=MESH)
    pl.semaphore_wait(barrier, len(peers))

    msgs = {}

    def send(name, b, src, dst, peer):
        i = len(msgs)
        copy = pltpu.make_async_remote_copy(
            src, dst, s["ssem"].at[i], s["rsem"].at[i], device_id=peer, device_id_type=MESH
        )
        copy.start()
        msgs[name, b] = copy

    def got(name, b):
        msgs[name, b].wait_recv()

    xa, hgu, part = s["xa"], s["hgu"], s["part"]

    def a1(b):
        xa[0, b, xi * NH + hi, ci] = x_ref[b * R : (b + 1) * R]
        xa[1, b, xi * NH + hi, ci] = c_ref[b * R : (b + 1) * R]
        mine = xa.at[:, b, xi * NH + hi, ci]
        send("a_h", b, mine, mine, at_h)
        for k in (1, 3, 2):
            send(f"a_x{k}", b, mine, mine, at_x(k))

    def a2(b):
        got("a_h", b)
        other = xa.at[:, b, xi * NH + h_o, ci]
        for k in (1, 3, 2):
            send(f"a_hx{k}", b, other, other, at_x(k))

    def a3(b):
        for k in (1, 3, 2):
            got(f"a_x{k}", b)
            got(f"a_hx{k}", b)
        same = xa.at[:, b, :, ci]
        send("a_c", b, same, same, at_c)

    def w(b):
        for load in loads:
            load.wait()

    def s1(b):
        got("a_c", b)
        p = b % 2
        x_all = xa[0, b].reshape(T, D)
        c_all = xa[1, b].reshape(T, D)
        part[p, 0] = nn(x_all, s["wg"][...]).reshape(NZ, NY, O, F)
        part[p, 1] = nn(x_all, s["wu"][...]).reshape(NZ, NY, O, F)
        for half, k in ((0, 1), (1, 3)):
            for i in range(2):
                s["far_s"][b, half, i] = part[p, i, zn(2), half].astype(BF16)
            send(f"far{half}", b, s["far_s"].at[b, half], s["far_r"].at[b, half], at_z(k))
        for way, k in ((0, 1), (1, 3)):
            for i in range(2):
                s["dir_s"][b, way, i] = part[p, i, zn(k), 1 - way].astype(BF16)
            send(f"dir{way}", b, s["dir_s"].at[b, way], s["dir_r"].at[b, way], at_z(k))
        part[p, 2] = nt(c_all, s["wd"][...]).reshape(NZ, NY, O, F)
        for z in range(NZ):
            s["sy_s"][b, z] = part[p, 2, z, y_o].astype(BF16)
        send("sy", b, s["sy_s"].at[b], s["sy_r"].at[b], at_y)

    def s2(b):
        p = b % 2
        for half, k in ((0, 1), (1, 3)):
            got(f"far{half}", b)
            for i in range(2):
                s["rel_s"][b, half, i] = (part[p, i, zn(k), half] + s["far_r"][b, half, i].astype(F32)).astype(BF16)
            send(f"rel{half}", b, s["rel_s"].at[b, half], s["rel_r"].at[b, half], at_z(k))

    def s3(b):
        p = b % 2
        got("sy", b)
        for k in (2, 1, 3):
            s["sz_s"][b, k - 1] = (part[p, 2, zn(k), yi] + s["sy_r"][b, zn(k)].astype(F32)).astype(BF16)
            send(f"sz{k}", b, s["sz_s"].at[b, k - 1], s["sz_r"].at[b, k - 1], at_z(k))
        s["s_own"][b] = part[p, 2, zi, yi] + s["sy_r"][b, zi].astype(F32)

    def s4(b):
        p = b % 2
        for half in range(2):
            got(f"dir{1 - half}", b)
            got(f"rel{half}", b)
            for i in range(2):
                s["zsum"][b, half, i] = (
                    part[p, i, zi, half]
                    + s["rel_r"][b, half, i].astype(F32)
                    + s["dir_r"][b, 1 - half, i].astype(F32)
                )
        send("gy", b, s["zsum"].at[b, y_o], s["gy_r"].at[b], at_y)

    def s5(b):
        got("gy", b)
        for k in (1, 2, 3):
            got(f"sz{k}", b)
        for j in range(0, O, 16):
            rows = slice(j, j + 16)
            gate = s["zsum"][b, yi, 0, rows] + s["gy_r"][b, 0, rows]
            up = s["zsum"][b, yi, 1, rows] + s["gy_r"][b, 1, rows]
            slope = s["s_own"][b, rows]
            for k in range(3):
                slope = slope + s["sz_r"][b, k, rows].astype(F32)
            sig = jax.nn.sigmoid(gate)
            act = gate * sig
            deriv = sig * (1.0 + gate * (1.0 - sig))
            hgu[0, b, zi, yi, rows] = (act * up).astype(BF16)
            hgu[1, b, zi, yi, rows] = (slope * up * deriv).astype(BF16)
            hgu[2, b, zi, yi, rows] = (slope * act).astype(BF16)
        mine = hgu.at[pl.ds(1, 2), b, zi, yi]
        send("c_y", b, mine, mine, at_y)
        mine = hgu.at[:, b, zi, yi]
        send("c_z1", b, mine, mine, at_z(1))
        send("c_z3", b, mine, mine, at_z(3))

    def s6a(b):
        got("c_y", b)
        other = hgu.at[pl.ds(1, 2), b, zi, y_o]
        send("c_yz1", b, other, other, at_z(1))
        send("c_yz3", b, other, other, at_z(3))

    def s6b(b):
        got("c_z1", b)
        below = hgu.at[pl.ds(1, 2), b, zn(3), yi]
        send("f_g1", b, below, below, at_z(1))
        below = hgu.at[0, b, zn(3), yi, pl.ds(0, O // 2)]
        send("f_h1", b, below, below, at_z(1))
        got("c_z3", b)
        above = hgu.at[0, b, zn(1), yi, pl.ds(O // 2, O // 2)]
        send("f_h3", b, above, above, at_z(3))

    def s6c(b):
        got("c_yz3", b)
        above = hgu.at[pl.ds(1, 2), b, zn(1), y_o]
        send("f_g3", b, above, above, at_z(3))
        got("c_yz1", b)

    def s7(b):
        got("f_h1", b)
        got("f_h3", b)
        mine = hgu.at[0, b, :, yi]
        send("h_y", b, mine, mine, at_y)

    def s8(b):
        got("f_g1", b)
        got("f_g3", b)
        gd = hgu[1, b].reshape(T, F)
        ud = hgu[2, b].reshape(T, F)
        s["igp"][b] = (nt(gd, s["wg"][...]) + nt(ud, s["wu"][...])).reshape(NX * NH, NC, R, D)
        send("co", b, s["igp"].at[b, :, c_o], s["co_r"].at[b], at_c)

    def s9(b):
        got("h_y", b)

    def s10(b):
        got("co", b)
        for k in (2, 1, 3):
            for h in range(NH):
                at = xn(k) * NH + h
                s["xs_s"][b, k - 1, h] = (s["igp"][b, at, ci] + s["co_r"][b, at]).astype(BF16)
            send(f"xs{k}", b, s["xs_s"].at[b, k - 1], s["xs_r"].at[b, k - 1], at_x(k))

    def s11(b):
        for k in (1, 3, 2):
            got(f"xs{k}", b)
        for h in range(NH):
            at = xi * NH + h
            total = s["igp"][b, at, ci] + s["co_r"][b, at]
            for k in range(3):
                total = total + s["xs_r"][b, k, h].astype(F32)
            s["igx"][b, h] = total
        send("h", b, s["igx"].at[b, h_o], s["h_r"].at[b], at_h)

    def s12(b):
        got("h", b)
        ig_ref[b * R : (b + 1) * R] = (s["igx"][b, hi] + s["h_r"][b]).astype(BF16)

    stores = []

    def g(step):
        head, tail = slice(0, NB - 1), slice(NB - 1, NB)
        n_head, n_tail = (NB - 1) * T, T
        if step == 0:
            x_h, c_h = xa[0, head].reshape(n_head, D), xa[1, head].reshape(n_head, D)
            s["acc_g"][...] = tn(x_h, hgu[1, head].reshape(n_head, F))
            s["acc_u"][...] = tn(x_h, hgu[2, head].reshape(n_head, F))
            s["acc_d"][...] = tn(hgu[0, head].reshape(n_head, F), c_h)
            return
        x_t, c_t = xa[0, tail].reshape(n_tail, D), xa[1, tail].reshape(n_tail, D)
        if step == 1:
            s["st_g"][...] = (s["acc_g"][...] + tn(x_t, hgu[1, tail].reshape(n_tail, F))).astype(BF16)
            out = (s["st_g"], gg_hbm)
        if step == 2:
            s["st_u"][...] = (s["acc_u"][...] + tn(x_t, hgu[2, tail].reshape(n_tail, F))).astype(BF16)
            out = (s["st_u"], ug_hbm)
        if step == 3:
            s["st_d"][...] = (s["acc_d"][...] + tn(hgu[0, tail].reshape(n_tail, F), c_t)).astype(BF16)
            out = (s["st_d"], dg_hbm)
        store = pltpu.make_async_copy(*out, s["lsem"].at[2 + step])
        store.start()
        stores.append(store)

    tasks = dict(a1=a1, a2=a2, a3=a3, w=w, s1=s1, s2=s2, s3=s3, s4=s4, s5=s5, s6a=s6a, s6b=s6b, s6c=s6c)
    tasks.update(s7=s7, s8=s8, s9=s9, s10=s10, s11=s11, s12=s12, g=g)
    for entry in ORDER:
        name, b = entry.split(":")
        tasks[name](int(b))

    for copy in msgs.values():
        copy.wait_send()
    for store in stores:
        store.wait()


def shards(x, c, wg, wu, wd):
    tokens, D = x.shape
    F = wg.shape[1]
    R = tokens // NB
    T = R * NX * NH * NC
    dims = {"D": D, "F": F, "T": T, "R": R, "O": T // (NZ * NY)}
    shapes = scratch(dims)
    vmem, anywhere = pl.BlockSpec(memory_space=pltpu.VMEM), pl.BlockSpec(memory_space=pl.ANY)
    names = tuple(shapes)

    def body(*refs):
        kernel(dims, names, *refs)

    return tuple(
        pl.pallas_call(
            body,
            name="swiglu_block",
            out_shape=[
                jax.ShapeDtypeStruct(x.shape, BF16),
                jax.ShapeDtypeStruct(wg.shape, BF16),
                jax.ShapeDtypeStruct(wu.shape, BF16),
                jax.ShapeDtypeStruct(wd.shape, BF16),
            ],
            in_specs=[vmem, vmem, anywhere, anywhere, anywhere],
            out_specs=[vmem, anywhere, anywhere, anywhere],
            scratch_shapes=list(shapes.values()),
            compiler_params=pltpu.CompilerParams(
                collective_id=0, has_side_effects=True, vmem_limit_bytes=62 * 2**20
            ),
            cost_estimate=pl.CostEstimate(
                flops=16 * NB * T * D * F, bytes_accessed=12 * D * F, transcendentals=0
            ),
        )(x, c, wg, wu, wd)
    )


def solution(mesh):
    placed = (P("col", "row"), P("col", "row"), P("row", "col"), P("row", "col"), P("col", "row"))
    return jax.shard_map(
        shards,
        mesh=mesh,
        in_specs=placed,
        out_specs=(P("col", "row"), P("row", "col"), P("row", "col"), P("col", "row")),
        check_vma=False,
    )
```

```python
import jax
import jax.numpy as jnp
from jax import lax
from jax.experimental import pallas as pl
from jax.experimental.pallas import tpu as pltpu
from jax.sharding import PartitionSpec as P

MESH = pl.DeviceIdType.MESH
F32, BF16 = jnp.float32, jnp.bfloat16
NZ, NY, NX, NH, NC = 4, 2, 4, 2, 2
STEPS = (0, 0, 1, 3, 2)
UNITS = ((0,), (1,), (2, 3), (4, 5), (6, 7))
FIRST = {1: 2, 3: 4, 2: 6}
CUT = 512

ORDER = (
    "aox:0", "axx:2", "aoc:0", "axc:3", "axx:3", "axc:2", "s1g:0", "ahx:0", "azx:2", "azx:3", "s1s:0", "s2:0",
    "ahc:0", "azc:2", "s1g:1", "azc:3", "axx:4", "acx:2", "s1s:1", "azx:4", "s3:0", "azc:4", "s4:0", "s2:1",
    "axc:4", "s1g:2", "acc:2", "acx:3", "s1s:2", "acc:3", "s2:2", "s1g:3", "s1s:3", "acx:4", "s4:2", "s3:2",
    "s2:3", "acc:4", "s1g:4", "s3b:2", "s1s:4", "s3b:0", "s4:3", "s2:4", "s3:4", "s5:2", "s4:4", "s3b:4",
    "s6a:2", "s3:3", "s5:4", "s3b:3", "s3:1", "s6a:4", "s4:1", "s6b:4", "s5:3", "s6c:4", "s5h:2", "s6a:3",
    "s5h:3", "s8:4", "s3b:1", "s6h:2", "s6b:2", "s6b:3", "s6c:2", "s10:4", "s6c:3", "s6h:3", "s5:0", "s5h:4",
    "s7:2", "s5h:0", "s5:1", "gg:3", "s5h:1", "s8:2", "s8:3", "s7:3", "gu:2", "s10:2", "s6h:4", "s9:2",
    "s10:3", "s6h:0", "s6a:0", "gg:1", "gg:2", "s6a:1", "s7:4", "s6h:1", "s6b:0", "gu:3", "s6c:0", "s9:3",
    "s7:0", "gd:1", "s6c:1", "s6b:1", "gu:1", "s8:0", "s7:1", "s8:1", "s9:4", "s10:0", "gg:0", "gd:2",
    "s10:1", "s9:0", "s11:0", "s9:1", "gd:0", "gd:3", "gu:0", "s12:0",
)


def nn(a, b):
    return lax.dot_general(a, b, (((1,), (0,)), ((), ())), preferred_element_type=F32)


def nt(a, b):
    return lax.dot_general(a, b, (((1,), (1,)), ((), ())), preferred_element_type=F32)


def tn(a, b):
    return lax.dot_general(a, b, (((0,), (0,)), ((), ())), preferred_element_type=F32)


def scratch(dims):
    D, F, R = dims["D"], dims["F"], dims["R"]
    U = NX * NH
    v = pltpu.VMEM
    shapes = {
        "wg": v((D, F), BF16),
        "wu": v((D, F), BF16),
        "wd": v((F, D), BF16),
        "xa": v((2, U, NC, R, D), BF16),
        "hgu": v((3, U * NC * R, F), BF16),
        "ig_o": v((U, R, D), F32),
        "ig_m": v((U, R, D), F32),
        "co_r": v((U, R, D), F32),
        "xs_r": v((U, R, D), F32),
        "h_s": v((R, D), BF16),
        "h_r": v((R, D), BF16),
        "acc_g": v((D, F), F32),
        "acc_u": v((D, F), F32),
        "acc_d": v((F, D), F32),
        "st_g": v((D, F), BF16),
        "st_u": v((D, F), BF16),
        "st_d": v((F, D), BF16),
        "ssem": pltpu.SemaphoreType.DMA((240,)),
        "rsem": pltpu.SemaphoreType.DMA((240,)),
        "lsem": pltpu.SemaphoreType.DMA((11,)),
    }
    for b, units in enumerate(UNITS):
        T = len(units) * NC * R
        O = T // (NZ * NY)
        if b < 4:
            shapes[f"part{b}"] = v((3, T, F), F32)
        for name in ("far_s", "far_r", "dir_s", "dir_r", "rel_s", "rel_r"):
            shapes[f"{name}{b}"] = v((2, 2, O, F), BF16)
        for name in ("gy_s", "gy_r"):
            shapes[f"{name}{b}"] = v((2, O, F), BF16)
        shapes[f"z_own{b}"] = v((2, O, F), F32)
        for name in ("sy_s", "sy_r"):
            shapes[f"{name}{b}"] = v((NZ * O, F), BF16)
        for name in ("sf_s", "sf_r", "sd_s", "sd_r", "sr_s", "sr_r"):
            shapes[f"{name}{b}"] = v((O, F), BF16)
        shapes[f"s_own{b}"] = v((O, F), F32)
    return shapes


def kernel(dims, names, x_hbm, c_hbm, wg_hbm, wu_hbm, wd_hbm, ig_ref, gg_hbm, ug_hbm, dg_hbm, *refs):
    D, F, R = dims["D"], dims["F"], dims["R"]
    s = dict(zip(names, refs))
    row, col = lax.axis_index("row"), lax.axis_index("col")
    yi, zi = row // NZ, row % NZ
    xi, hi, ci = col // (NH * NC), (col // NC) % NH, col % NC
    y_o = 1 - yi

    def zn(k):
        return (zi + k) % NZ

    def at_z(k):
        return (yi * NZ + zn(k), col)

    def at_x(k):
        return (row, ((xi + k) % NX) * (NH * NC) + hi * NC + ci)

    at_y = (y_o * NZ + zi, col)
    at_h = (row, xi * (NH * NC) + (1 - hi) * NC + ci)
    at_c = (row, xi * (NH * NC) + hi * NC + 1 - ci)
    xa, hgu = s["xa"], s["hgu"]
    low, high = pl.ds(0, CUT), pl.ds(CUT, F - CUT)

    def tokens(b):
        return len(UNITS[b]) * NC * R

    def owned(b):
        return tokens(b) // (NZ * NY)

    def start(b):
        return UNITS[b][0] * NC * R

    def rows(b, y, z, count=1):
        O = owned(b)
        return pl.ds(pl.multiple_of((y * NZ + z) * O, O), O * count)

    def all_rows(b, y, z, count=1):
        O = owned(b)
        return pl.ds(pl.multiple_of(start(b) + (y * NZ + z) * O, O), O * count)

    def part(b):
        return s[f"part{2 if b == 4 else b}"]

    loads = [
        pltpu.make_async_copy(src, dst, s["lsem"].at[i])
        for i, (src, dst) in enumerate(
            (
                (x_hbm, xa.at[0, 0, 0]),
                (c_hbm, xa.at[1, 0, 0]),
                (wg_hbm, s["wg"]),
                (wu_hbm, s["wu"]),
                (wd_hbm, s["wd"]),
            )
        )
    ]
    for load in loads:
        load.start()

    barrier = pltpu.get_barrier_semaphore()
    peers = [at_c, at_h, at_y, at_z(1), at_z(3), at_x(1), at_x(3), at_x(2)]
    for peer in peers:
        pl.semaphore_signal(barrier, inc=1, device_id=peer, device_id_type=MESH)
    pl.semaphore_wait(barrier, len(peers))

    msgs = {}

    def send(name, b, src, dst, peer):
        i = len(msgs)
        copy = pltpu.make_async_remote_copy(
            src, dst, s["ssem"].at[i], s["rsem"].at[i], device_id=peer, device_id_type=MESH
        )
        copy.start()
        msgs[name, b] = copy

    def got(name, b):
        msgs[name, b].wait_recv()

    def gather(tag, a):
        def own(b):
            loads[a].wait()
            send(f"aC{tag}", 0, xa.at[a, 0, 0], xa.at[a, 0, 1], at_c)
            send(f"ah{tag}", 0, xa.at[a, 0, 0], xa.at[a, 1, 0], at_h)

        def out(b):
            k = STEPS[b]
            send(f"ax{tag}", b, xa.at[a, 0, 0], xa.at[a, FIRST[k], 0], at_x(-k % NX))

        def across(b):
            got(f"ah{tag}", 0)
            send(f"aC{tag}", 1, xa.at[a, 1, 0], xa.at[a, 1, 1], at_c)

        def on(b):
            k = STEPS[b]
            send(f"az{tag}", b, xa.at[a, 1, 0], xa.at[a, FIRST[k] + 1, 0], at_x(-k % NX))

        def twin(b):
            got(f"ax{tag}", b)
            got(f"az{tag}", b)
            here = pl.ds(UNITS[b][0], 2)
            send(f"aC{tag}", b, xa.at[a, here, 0], xa.at[a, here, 1], at_c)

        return {f"ao{tag}": own, f"ax{tag}": out, f"ah{tag}": across, f"az{tag}": on, f"ac{tag}": twin}

    def block(ref, b):
        return ref[UNITS[b][0] : UNITS[b][-1] + 1].reshape(tokens(b), D)

    def s1g(b):
        got("aCx", b)
        if b == 0:
            loads[2].wait()
            loads[3].wait()
        p = part(b)
        x_all = block(xa.at[0], b)
        p[0] = nn(x_all, s["wg"][...])
        p[1] = nn(x_all, s["wu"][...])
        for half, k in ((0, 1), (1, 3)):
            for i in range(2):
                s[f"far_s{b}"][half, i] = p[i, rows(b, half, zn(2))].astype(BF16)
            send(f"far{half}", b, s[f"far_s{b}"].at[half], s[f"far_r{b}"].at[half], at_z(k))
        for way, k in ((0, 1), (1, 3)):
            for i in range(2):
                s[f"dir_s{b}"][way, i] = p[i, rows(b, 1 - way, zn(k))].astype(BF16)
            send(f"dir{way}", b, s[f"dir_s{b}"].at[way], s[f"dir_r{b}"].at[way], at_z(k))

    def s1s(b):
        got("aCc", b)
        if b == 0:
            loads[4].wait()
        p = part(b)
        p[2] = nt(block(xa.at[1], b), s["wd"][...])
        s[f"sy_s{b}"][...] = p[2, rows(b, y_o, 0, NZ)].astype(BF16)
        send("sy", b, s[f"sy_s{b}"], s[f"sy_r{b}"], at_y)

    def s2(b):
        for half, k in ((0, 1), (1, 3)):
            got(f"far{half}", b)
            for i in range(2):
                total = part(b)[i, rows(b, half, zn(k))] + s[f"far_r{b}"][half, i].astype(F32)
                s[f"rel_s{b}"][half, i] = total.astype(BF16)
            send(f"rel{half}", b, s[f"rel_s{b}"].at[half], s[f"rel_r{b}"].at[half], at_z(k))

    def pair(b, k, cols):
        return part(b)[2, rows(b, yi, zn(k)), cols] + s[f"sy_r{b}"][rows(b, 0, zn(k)), cols].astype(F32)

    def send_slope(name, b, cols, way, k):
        src, dst = s[f"{name}_s{b}"].at[:, cols], s[f"{name}_r{b}"].at[:, cols]
        send(f"{name}{way}", b, src, dst, at_z(k))

    def s3(b):
        got("sy", b)
        s[f"sf_s{b}"][...] = pair(b, 2, slice(None)).astype(BF16)
        send_slope("sf", b, low, 0, 1)
        send_slope("sf", b, high, 1, 3)
        s[f"sd_s{b}"][:, high] = pair(b, 1, high).astype(BF16)
        send_slope("sd", b, high, 0, 1)
        s[f"sd_s{b}"][:, low] = pair(b, 3, low).astype(BF16)
        send_slope("sd", b, low, 1, 3)
        s[f"s_own{b}"][...] = pair(b, 0, slice(None))

    def s3b(b):
        for way, k, cols in ((0, 1, low), (1, 3, high)):
            got(f"sf{way}", b)
            s[f"sr_s{b}"][:, cols] = (pair(b, k, cols) + s[f"sf_r{b}"][:, cols].astype(F32)).astype(BF16)
            send_slope("sr", b, cols, way, k)

    def s4(b):
        for half in range(2):
            got(f"dir{1 - half}", b)
            got(f"rel{half}", b)

        def total(i, y):
            here = part(b)[i, rows(b, y, zi)]
            return here + s[f"rel_r{b}"][y, i].astype(F32) + s[f"dir_r{b}"][1 - y, i].astype(F32)

        for i in range(2):
            s[f"gy_s{b}"][i] = total(i, y_o).astype(BF16)
        send("gy", b, s[f"gy_s{b}"], s[f"gy_r{b}"], at_y)
        for i in range(2):
            s[f"z_own{b}"][i] = total(i, yi)

    def s5(b):
        got("gy", b)
        for way in range(2):
            got(f"sr{way}", b)
            got(f"sd{way}", b)
        for j in range(0, owned(b), 16):
            at = slice(j, j + 16)
            gate = s[f"z_own{b}"][0, at] + s[f"gy_r{b}"][0, at].astype(F32)
            up = s[f"z_own{b}"][1, at] + s[f"gy_r{b}"][1, at].astype(F32)
            slope = s[f"s_own{b}"][at] + s[f"sr_r{b}"][at].astype(F32) + s[f"sd_r{b}"][at].astype(F32)
            sig = jax.nn.sigmoid(gate)
            act = gate * sig
            deriv = sig * (1.0 + gate * (1.0 - sig))
            to = pl.ds(pl.multiple_of(start(b) + (yi * NZ + zi) * owned(b) + j, 16), 16)
            hgu[0, to] = (act * up).astype(BF16)
            hgu[1, to] = (slope * up * deriv).astype(BF16)
            hgu[2, to] = (slope * act).astype(BF16)
        mine = hgu.at[pl.ds(1, 2), all_rows(b, yi, zi)]
        send("c_y", b, mine, mine, at_y)
        send("c_z1", b, mine, mine, at_z(1))
        send("c_z3", b, mine, mine, at_z(3))

    def s5h(b):
        mine = hgu.at[0, all_rows(b, yi, zi)]
        send("h_z1", b, mine, mine, at_z(1))
        send("h_z3", b, mine, mine, at_z(3))

    def s6a(b):
        got("c_y", b)
        other = hgu.at[pl.ds(1, 2), all_rows(b, y_o, zi)]
        send("c_yz1", b, other, other, at_z(1))
        send("c_yz3", b, other, other, at_z(3))

    def s6b(b):
        got("c_z1", b)
        below = hgu.at[pl.ds(1, 2), all_rows(b, yi, zn(3))]
        send("f_g1", b, below, below, at_z(1))
        got("c_z3", b)

    def s6c(b):
        got("c_yz3", b)
        above = hgu.at[pl.ds(1, 2), all_rows(b, y_o, zn(1))]
        send("f_g3", b, above, above, at_z(3))
        got("c_yz1", b)

    def s6h(b):
        got("h_z1", b)
        below = hgu.at[0, all_rows(b, yi, zn(3)), low]
        send("f_h1", b, below, below, at_z(1))
        got("h_z3", b)
        above = hgu.at[0, all_rows(b, yi, zn(1)), high]
        send("f_h3", b, above, above, at_z(3))

    def s7(b):
        got("f_h1", b)
        got("f_h3", b)
        mine = hgu.at[0, all_rows(b, yi, 0, NZ)]
        send("h_y", b, mine, mine, at_y)

    def s8(b):
        got("f_g1", b)
        got("f_g3", b)
        n = len(UNITS[b])
        here = pl.ds(UNITS[b][0], n)

        def of_core(core):
            at = slice(start(b), start(b) + tokens(b))
            gd = hgu[1, at].reshape(n, NC, R, F)[:, core].reshape(n * R, F)
            ud = hgu[2, at].reshape(n, NC, R, F)[:, core].reshape(n * R, F)
            return (nt(gd, s["wg"][...]) + nt(ud, s["wu"][...])).reshape(n, R, D)

        s["ig_o"][here] = of_core(1)
        send("co", b, s["ig_o"].at[here], s["co_r"].at[here], at_c)
        s["ig_m"][here] = of_core(0)

    def s9(b):
        got("h_y", b)

    def s10(b):
        got("co", b)
        here = pl.ds(UNITS[b][0], len(UNITS[b]))
        s["ig_m"][here] += s["co_r"][here]
        if b >= 2:
            k = STEPS[b]
            send("xs", b, s["ig_m"].at[here], s["xs_r"].at[pl.ds(FIRST[-k % NX], 2)], at_x(k))

    def gathered(unit):
        total = s["ig_m"][unit]
        for k in (1, 3, 2):
            total = total + s["xs_r"][FIRST[k] + unit]
        return total

    def s11(b):
        for step in (2, 3, 4):
            got("xs", step)
        s["h_s"][...] = gathered(1).astype(BF16)
        send("h", 0, s["h_s"], s["h_r"], at_h)

    def s12(b):
        mine = gathered(0)
        got("h", 0)
        ig_ref[...] = (mine + s["h_r"][...].astype(F32)).astype(BF16)

    spans = (slice(0, 2), slice(2, 4), slice(4, 6), slice(6, 8))
    stores = []

    def grad(left, right, acc, stage, out):
        seen = []

        def g(step):
            seen.append(step)
            if len(seen) == 1:
                acc[...] = tn(left(step), right(step))
            elif len(seen) < len(spans):
                acc[...] += tn(left(step), right(step))
            else:
                half = stage.shape[0] // 2
                for at in (pl.ds(0, half), pl.ds(half, half)):
                    stage[at] = (acc[at] + tn(left(step, at), right(step))).astype(BF16)
                    store = pltpu.make_async_copy(stage.at[at], out.at[at], s["lsem"].at[5 + len(stores)])
                    store.start()
                    stores.append(store)

        return g

    def activations(a):
        def pick(step, at=slice(None)):
            return xa[a, spans[step], :, :, at].reshape(-1, D if isinstance(at, slice) else at.size)

        return pick

    def results(a):
        def pick(step, at=slice(None)):
            return hgu[a, spans[step].start * NC * R : spans[step].stop * NC * R, at]

        return pick

    tasks = gather("x", 0) | gather("c", 1)
    tasks.update(s1g=s1g, s1s=s1s, s2=s2, s3=s3, s3b=s3b, s4=s4, s5=s5, s5h=s5h, s6a=s6a, s6b=s6b, s6c=s6c)
    tasks.update(s6h=s6h, s7=s7, s8=s8, s9=s9, s10=s10, s11=s11, s12=s12)
    tasks["gg"] = grad(activations(0), results(1), s["acc_g"], s["st_g"], gg_hbm)
    tasks["gu"] = grad(activations(0), results(2), s["acc_u"], s["st_u"], ug_hbm)
    tasks["gd"] = grad(results(0), activations(1), s["acc_d"], s["st_d"], dg_hbm)
    for entry in ORDER:
        name, b = entry.split(":")
        tasks[name](int(b))

    for copy in msgs.values():
        copy.wait_send()
    for store in stores:
        store.wait()


def place(*refs):
    n = 4
    src, dst, buf, (sem_in, sem_out) = refs[:n], refs[n : 2 * n], refs[2 * n : 3 * n], refs[3 * n :]
    moves = []
    for a in range(n):
        pieces = 2 if a else 1
        rows = src[a].shape[0] // pieces
        for j in range(pieces):
            at, i = pl.ds(j * rows, rows), len(moves)
            come = pltpu.make_async_copy(src[a].at[at], buf[a].at[at], sem_in.at[i])
            come.start()
            moves.append((come, pltpu.make_async_copy(buf[a].at[at], dst[a].at[at], sem_out.at[i])))
    for come, go in moves:
        come.wait()
        go.start()
    for _, go in moves:
        go.wait()


def shards(x, c, wg, wu, wd):
    R, D = x.shape
    F = wg.shape[1]
    dims = {"D": D, "F": F, "R": R}
    shapes = scratch(dims)
    vmem, anywhere = pl.BlockSpec(memory_space=pltpu.VMEM), pl.BlockSpec(memory_space=pl.ANY)
    names = tuple(shapes)

    def body(*refs):
        kernel(dims, names, *refs)

    out_shape = [jax.ShapeDtypeStruct(a.shape, BF16) for a in (x, wg, wu, wd)]
    outs = pl.pallas_call(
        body,
        name="swiglu_block",
        out_shape=out_shape,
        in_specs=[anywhere] * 5,
        out_specs=[vmem, anywhere, anywhere, anywhere],
        scratch_shapes=list(shapes.values()),
        compiler_params=pltpu.CompilerParams(collective_id=0, has_side_effects=True, vmem_limit_bytes=62 * 2**20),
        cost_estimate=pl.CostEstimate(flops=16 * NX * NH * NC * R * D * F, bytes_accessed=12 * D * F, transcendentals=0),
    )(x, c, wg, wu, wd)
    return tuple(
        pl.pallas_call(
            place,
            name="place_outputs",
            out_shape=out_shape,
            in_specs=[anywhere] * 4,
            out_specs=[anywhere] * 4,
            scratch_shapes=[pltpu.VMEM(a.shape, BF16) for a in out_shape] + [pltpu.SemaphoreType.DMA((8,))] * 2,
            compiler_params=pltpu.CompilerParams(vmem_limit_bytes=62 * 2**20),
            cost_estimate=pl.CostEstimate(flops=0, bytes_accessed=12 * D * F, transcendentals=0),
        )(*outs)
    )


def solution(mesh):
    placed = (P("col", "row"), P("col", "row"), P("row", "col"), P("row", "col"), P("col", "row"))
    return jax.shard_map(
        shards,
        mesh=mesh,
        in_specs=placed,
        out_specs=(P("col", "row"), P("row", "col"), P("row", "col"), P("col", "row")),
        check_vma=False,
    )
```

```python
import jax
import jax.numpy as jnp
from jax import lax
from jax.experimental import pallas as pl
from jax.experimental.pallas import tpu as pltpu
from jax.sharding import PartitionSpec as P

MESH = pl.DeviceIdType.MESH
F32, BF16 = jnp.float32, jnp.bfloat16
NZ, NY, NX, NH, NC = 4, 2, 4, 2, 2
PLACE = ((0, 0), (0, 1), (1, 0), (3, 0), (1, 1), (3, 1), (2, 0), (2, 1))
UNITS = ((0,), (1,), (2, 3), (4, 5), (6, 7))
SPANS = ((0, 2), (2, 4), (4, 6), (6, 8))
HIDDEN_Y_FIRST = (0, 1, 4)
CUT = 512
ORDER = (
    0, 13, 12, 40, 52, 53, 80, 90, 16, 20, 32, 14, 15, 17, 100, 81, 72, 60, 54, 82, 55, 130, 56, 91, 57, 92,
    33, 102, 83, 73, 34, 132, 93, 112, 84, 74, 103, 122, 94, 104, 113, 142, 114, 152, 134, 133, 124, 110, 162,
    123, 144, 154, 172, 182, 143, 164, 174, 153, 192, 252, 184, 120, 101, 301, 291, 111, 202, 163, 262, 194,
    254, 131, 140, 121, 150, 264, 212, 303, 173, 183, 203, 141, 151, 160, 293, 222, 161, 193, 253, 213, 170,
    171, 200, 292, 180, 263, 181, 201, 210, 242, 204, 223, 302, 190, 250, 191, 211, 251, 214, 221, 290, 260,
    230, 220, 261, 270, 224, 231, 311, 234, 300, 243, 312, 241, 240, 310, 244, 313, 280,
)


def nn(a, b):
    return lax.dot_general(a, b, (((1,), (0,)), ((), ())), preferred_element_type=F32)


def nt(a, b):
    return lax.dot_general(a, b, (((1,), (1,)), ((), ())), preferred_element_type=F32)


def tn(a, b):
    return lax.dot_general(a, b, (((0,), (0,)), ((), ())), preferred_element_type=F32)


def scratch(dims):
    D, F, R = dims["D"], dims["F"], dims["R"]
    U = NX * NH
    v = pltpu.VMEM
    shapes = {
        "wg": v((D, F), BF16),
        "wu": v((D, F), BF16),
        "wd": v((F, D), BF16),
        "xa": v((2, U, NC, R, D), BF16),
        "hgu": v((3, U * NC * R, F), BF16),
        "ig_o": v((U, R, D), F32),
        "ig_m": v((U, R, D), F32),
        "co_r": v((U, R, D), F32),
        "xs_r": v((U, R, D), F32),
        "h_s": v((R, D), BF16),
        "h_r": v((R, D), BF16),
        "acc_g": v((D, F), F32),
        "acc_u": v((D, F), F32),
        "acc_d": v((F, D), F32),
        "st_g": v((D, F), BF16),
        "st_u": v((D, F), BF16),
        "st_d": v((F, D), BF16),
        "ssem": pltpu.SemaphoreType.DMA((240,)),
        "rsem": pltpu.SemaphoreType.DMA((240,)),
        "lsem": pltpu.SemaphoreType.DMA((11,)),
    }
    for b, units in enumerate(UNITS):
        T = len(units) * NC * R
        O = T // (NZ * NY)
        if b < 4:
            shapes["part", b] = v((3, T, F), F32)
        for name in ("far", "dir", "rel"):
            shapes[name, 0, b] = shapes[name, 1, b] = v((2, 2, O, F), BF16)
        shapes["ry", 0, b] = shapes["ry", 1, b] = v((2, O, F), BF16)
        shapes["sy", 0, b] = shapes["sy", 1, b] = v((NZ * O, F), BF16)
        for name in ("sf", "sd", "sr"):
            shapes[name, 0, b] = shapes[name, 1, b] = v((O, F), BF16)
        shapes["z_own", b] = v((2, O, F), F32)
        shapes["s_own", b] = v((O, F), F32)
    return shapes


def kernel(dims, names, x_hbm, c_hbm, wg_hbm, wu_hbm, wd_hbm, ig_ref, gg_hbm, ug_hbm, dg_hbm, *refs):
    D, F, R = dims["D"], dims["F"], dims["R"]
    s = dict(zip(names, refs))
    row, col = lax.axis_index("row"), lax.axis_index("col")
    yi, zi = row // NZ, row % NZ
    xi, hi, ci = col // (NH * NC), (col // NC) % NH, col % NC
    y_o = 1 - yi

    def zn(k):
        return (zi + k) % NZ

    def at_z(k):
        return (yi * NZ + zn(k), col)

    def at_x(k):
        return (row, ((xi + k) % NX) * (NH * NC) + hi * NC + ci)

    at_y = (y_o * NZ + zi, col)
    at_h = (row, xi * (NH * NC) + (1 - hi) * NC + ci)
    at_c = (row, xi * (NH * NC) + hi * NC + 1 - ci)
    xa, hgu = s["xa"], s["hgu"]
    low, high = pl.ds(0, CUT), pl.ds(CUT, F - CUT)
    ways = ((0, 1), (1, 3))

    def back(u):
        k, h = PLACE[u]
        return PLACE.index((-k % NX, h)), k

    def tokens(b):
        return len(UNITS[b]) * NC * R

    def owned(b):
        return tokens(b) // (NZ * NY)

    def start(b):
        return UNITS[b][0] * NC * R

    def rows(b, y, z, count=1):
        O = owned(b)
        return pl.ds(pl.multiple_of((y * NZ + z) * O, O), O * count)

    def all_rows(b, y, z, count=1):
        O = owned(b)
        return pl.ds(pl.multiple_of(start(b) + (y * NZ + z) * O, O), O * count)

    def part(b):
        return s["part", b if b < 4 else b - 2]

    loads = [
        pltpu.make_async_copy(src, dst, s["lsem"].at[i])
        for i, (src, dst) in enumerate(
            (
                (x_hbm, xa.at[0, 0, 0]),
                (c_hbm, xa.at[1, 0, 0]),
                (wg_hbm, s["wg"]),
                (wu_hbm, s["wu"]),
                (wd_hbm, s["wd"]),
            )
        )
    ]
    for load in loads:
        load.start()

    barrier = pltpu.get_barrier_semaphore()
    peers = [at_c, at_h, at_y, at_z(1), at_z(3), at_x(1), at_x(3), at_x(2)]
    for peer in peers:
        pl.semaphore_signal(barrier, inc=1, device_id=peer, device_id_type=MESH)
    pl.semaphore_wait(barrier, len(peers))

    msgs = {}

    def send(key, src, dst, peer):
        i = len(msgs)
        copy = pltpu.make_async_remote_copy(
            src, dst, s["ssem"].at[i], s["rsem"].at[i], device_id=peer, device_id_type=MESH
        )
        copy.start()
        msgs[key] = copy

    def got(*key):
        msgs[key].wait_recv()

    def gather(a):
        def own(b):
            loads[a].wait()
            send(("aC", a, 0), xa.at[a, 0, 0], xa.at[a, 0, 1], at_c)
            send(("ah", a), xa.at[a, 0, 0], xa.at[a, 1, 0], at_h)

        def along(u):
            there, k = back(u)
            src = xa.at[a, PLACE[u][1], 0]
            send(("ax", a, there), src, xa.at[a, there, 0], at_x(k))

        def across(b):
            got("ah", a)
            send(("aC", a, 1), xa.at[a, 1, 0], xa.at[a, 1, 1], at_c)

        def twin(b):
            for u in UNITS[b]:
                got("ax", a, u)
            here = pl.ds(UNITS[b][0], len(UNITS[b]))
            send(("aC", a, b), xa.at[a, here, 0], xa.at[a, here, 1], at_c)

        return [own, along, across, twin]

    def block(a, b):
        return xa[a, UNITS[b][0] : UNITS[b][-1] + 1].reshape(tokens(b), D)

    def send_z(name, b, way, k, dims=()):
        at = dims or (way,)
        send((name, way, b), s[name, 0, b].at[at], s[name, 1, b].at[at], at_z(k))

    def s1g(b):
        got("aC", 0, b)
        if b == 0:
            loads[2].wait()
            loads[3].wait()
        p = part(b)
        x_all = block(0, b)
        p[0] = nn(x_all, s["wg"][...])
        p[1] = nn(x_all, s["wu"][...])
        for half, k in ways:
            for i in range(2):
                s["far", 0, b][half, i] = p[i, rows(b, half, zn(2))].astype(BF16)
            send_z("far", b, half, k)
        for way, k in ways:
            for i in range(2):
                s["dir", 0, b][way, i] = p[i, rows(b, 1 - way, zn(k))].astype(BF16)
            send_z("dir", b, way, k)

    def s1s(b):
        got("aC", 1, b)
        if b == 0:
            loads[4].wait()
        p = part(b)
        p[2] = nt(block(1, b), s["wd"][...])
        s["sy", 0, b][...] = p[2, rows(b, y_o, 0, NZ)].astype(BF16)
        send(("sy", b), s["sy", 0, b], s["sy", 1, b], at_y)

    def s2(b):
        for half, k in ways:
            got("far", half, b)
            for i in range(2):
                total = part(b)[i, rows(b, half, zn(k))] + s["far", 1, b][half, i].astype(F32)
                s["rel", 0, b][half, i] = total.astype(BF16)
            send_z("rel", b, half, k)

    def pair(b, k, cols):
        return part(b)[2, rows(b, yi, zn(k)), cols] + s["sy", 1, b][rows(b, 0, zn(k)), cols].astype(F32)

    every = slice(None)

    def s3(b):
        got("sy", b)
        s["sf", 0, b][...] = pair(b, 2, every).astype(BF16)
        send_z("sf", b, 0, 1, (every, low))
        send_z("sf", b, 1, 3, (every, high))
        s["sd", 0, b][:, high] = pair(b, 1, high).astype(BF16)
        send_z("sd", b, 0, 1, (every, high))
        s["sd", 0, b][:, low] = pair(b, 3, low).astype(BF16)
        send_z("sd", b, 1, 3, (every, low))
        s["s_own", b][...] = pair(b, 0, every)

    def s3b(b):
        for way, k, cols in ((0, 1, low), (1, 3, high)):
            got("sf", way, b)
            s["sr", 0, b][:, cols] = (pair(b, k, cols) + s["sf", 1, b][:, cols].astype(F32)).astype(BF16)
            send_z("sr", b, way, k, (every, cols))

    def s4(b):
        for half in range(2):
            got("dir", 1 - half, b)
            got("rel", half, b)

        def total(i, y):
            here = part(b)[i, rows(b, y, zi)]
            return here + s["rel", 1, b][y, i].astype(F32) + s["dir", 1, b][1 - y, i].astype(F32)

        for i in range(2):
            s["ry", 0, b][i] = total(i, y_o).astype(BF16)
        send(("ry", b), s["ry", 0, b], s["ry", 1, b], at_y)
        for i in range(2):
            s["z_own", b][i] = total(i, yi)

    def s5(b):
        got("ry", b)
        for way in range(2):
            got("sr", way, b)
            got("sd", way, b)
        for j in range(0, owned(b), 16):
            at = slice(j, j + 16)
            gate = s["z_own", b][0, at] + s["ry", 1, b][0, at].astype(F32)
            up = s["z_own", b][1, at] + s["ry", 1, b][1, at].astype(F32)
            slope = s["s_own", b][at] + s["sr", 1, b][at].astype(F32) + s["sd", 1, b][at].astype(F32)
            sig = jax.nn.sigmoid(gate)
            act = gate * sig
            deriv = sig * (1.0 + gate * (1.0 - sig))
            to = pl.ds(pl.multiple_of(start(b) + (yi * NZ + zi) * owned(b) + j, 16), 16)
            hgu[0, to] = (act * up).astype(BF16)
            hgu[1, to] = (slope * up * deriv).astype(BF16)
            hgu[2, to] = (slope * act).astype(BF16)

    def spread(first, count, y_first):
        arrays = pl.ds(first, count)

        def put(name, way, b, at, peer):
            here = hgu.at[(arrays,) + at]
            send((name, way, b, first), here, here, peer)

        def begin(b):
            mine = (all_rows(b, yi, zi),)
            if b in y_first:
                put("cy", 0, b, mine, at_y)
            for way, k in ways:
                put("cz", way, b, mine, at_z(k))

        def second(b):
            if b in y_first:
                got("cy", 0, b, first)
                for way, k in ways:
                    put("cu", way, b, (all_rows(b, y_o, zi),), at_z(k))
            else:
                for way, k, cols in ((0, 1, low), (1, 3, high)):
                    got("cz", way, b, first)
                    put("cf", way, b, (all_rows(b, yi, zn(-k % NZ)), cols), at_z(k))

        def third(b):
            if b in y_first:
                got("cz", 0, b, first)
                put("cf", 0, b, (all_rows(b, yi, zn(3)),), at_z(1))
                got("cz", 1, b, first)
            else:
                got("cf", 0, b, first)
                got("cf", 1, b, first)
                put("cy", 0, b, (all_rows(b, yi, 0, NZ),), at_y)

        def fourth(b):
            got("cu", 1, b, first)
            put("cf", 1, b, (all_rows(b, y_o, zn(1)),), at_z(3))
            got("cu", 0, b, first)

        def last(b):
            if b in y_first:
                got("cf", 0, b, first)
                got("cf", 1, b, first)
            else:
                got("cy", 0, b, first)

        return [begin, second, third, fourth, last]

    def s8(b):
        n = len(UNITS[b])
        here = pl.ds(UNITS[b][0], n)

        def of_core(core):
            at = slice(start(b), start(b) + tokens(b))
            gd = hgu[1, at].reshape(n, NC, R, F)[:, core].reshape(n * R, F)
            ud = hgu[2, at].reshape(n, NC, R, F)[:, core].reshape(n * R, F)
            return (nt(gd, s["wg"][...]) + nt(ud, s["wu"][...])).reshape(n, R, D)

        s["ig_o"][here] = of_core(1)
        send(("co", b), s["ig_o"].at[here], s["co_r"].at[here], at_c)
        s["ig_m"][here] = of_core(0)

    def s10(b):
        got("co", b)
        here = pl.ds(UNITS[b][0], len(UNITS[b]))
        s["ig_m"][here] += s["co_r"][here]
        if b >= 2:
            for u in UNITS[b]:
                there, k = back(u)
                send(("xs", there), s["ig_m"].at[u], s["xs_r"].at[there], at_x(k))

    def gathered(h):
        total = s["ig_m"][h]
        for u, (k, other) in enumerate(PLACE):
            if k and other == h:
                total = total + s["xs_r"][u]
        return total

    def s11(b):
        for u in range(2, len(PLACE)):
            got("xs", u)
        s["h_s"][...] = gathered(1).astype(BF16)
        send(("h",), s["h_s"], s["h_r"], at_h)

    def s12(b):
        mine = gathered(0)
        got("h")
        ig_ref[...] = (mine + s["h_r"][...].astype(F32)).astype(BF16)

    stores = []

    def grad(left, right, acc, stage, out):
        seen = []

        def g(step):
            seen.append(step)
            if len(seen) == 1:
                acc[...] = tn(left(step), right(step))
            elif len(seen) < len(SPANS):
                acc[...] += tn(left(step), right(step))
            else:
                half = stage.shape[0] // 2
                for at in (pl.ds(0, half), pl.ds(half, half)):
                    stage[at] = (acc[at] + tn(left(step, at), right(step))).astype(BF16)
                    store = pltpu.make_async_copy(stage.at[at], out.at[at], s["lsem"].at[5 + len(stores)])
                    store.start()
                    stores.append(store)

        return g

    def activations(a):
        def pick(step, at=pl.ds(0, D)):
            first, end = SPANS[step]
            return xa[a, first:end, :, :, at].reshape(-1, at.size)

        return pick

    def results(a):
        def pick(step, at=pl.ds(0, F)):
            first, end = SPANS[step]
            return hgu[a, first * NC * R : end * NC * R, at]

        return pick

    tasks = [*gather(0), *gather(1), s1g, s1s, s2, s3, s3b, s4, s5]
    tasks += [*spread(1, 2, range(len(UNITS))), *spread(0, 1, HIDDEN_Y_FIRST), s8, s10, s11, s12]
    tasks.append(grad(activations(0), results(1), s["acc_g"], s["st_g"], gg_hbm))
    tasks.append(grad(activations(0), results(2), s["acc_u"], s["st_u"], ug_hbm))
    tasks.append(grad(results(0), activations(1), s["acc_d"], s["st_d"], dg_hbm))
    for entry in ORDER:
        tasks[entry // 10](entry % 10)

    for copy in msgs.values():
        copy.wait_send()
    for store in stores:
        store.wait()


def place(*refs):
    n = 4
    src, dst, buf, (sem_in, sem_out) = refs[:n], refs[n : 2 * n], refs[2 * n : 3 * n], refs[3 * n :]
    moves = []
    for a in range(n):
        pieces = 2 if a else 1
        rows = src[a].shape[0] // pieces
        for j in range(pieces):
            at, i = pl.ds(j * rows, rows), len(moves)
            come = pltpu.make_async_copy(src[a].at[at], buf[a].at[at], sem_in.at[i])
            come.start()
            moves.append((come, pltpu.make_async_copy(buf[a].at[at], dst[a].at[at], sem_out.at[i])))
    for come, go in moves:
        come.wait()
        go.start()
    for _, go in moves:
        go.wait()


def shards(x, c, wg, wu, wd):
    R, D = x.shape
    F = wg.shape[1]
    dims = {"D": D, "F": F, "R": R}
    shapes = scratch(dims)
    vmem, anywhere = pl.BlockSpec(memory_space=pltpu.VMEM), pl.BlockSpec(memory_space=pl.ANY)
    names = tuple(shapes)

    def body(*refs):
        kernel(dims, names, *refs)

    out_shape = [jax.ShapeDtypeStruct(a.shape, BF16) for a in (x, wg, wu, wd)]
    outs = pl.pallas_call(
        body,
        name="swiglu_block",
        out_shape=out_shape,
        in_specs=[anywhere] * 5,
        out_specs=[vmem, anywhere, anywhere, anywhere],
        scratch_shapes=list(shapes.values()),
        compiler_params=pltpu.CompilerParams(collective_id=0, has_side_effects=True, vmem_limit_bytes=62 * 2**20),
        cost_estimate=pl.CostEstimate(flops=16 * NX * NH * NC * R * D * F, bytes_accessed=12 * D * F, transcendentals=0),
    )(x, c, wg, wu, wd)
    return tuple(
        pl.pallas_call(
            place,
            name="place_outputs",
            out_shape=out_shape,
            in_specs=[anywhere] * 4,
            out_specs=[anywhere] * 4,
            scratch_shapes=[pltpu.VMEM(a.shape, BF16) for a in out_shape] + [pltpu.SemaphoreType.DMA((8,))] * 2,
            compiler_params=pltpu.CompilerParams(vmem_limit_bytes=62 * 2**20),
            cost_estimate=pl.CostEstimate(flops=0, bytes_accessed=12 * D * F, transcendentals=0),
        )(*outs)
    )


def solution(mesh):
    placed = (P("col", "row"), P("col", "row"), P("row", "col"), P("row", "col"), P("col", "row"))
    return jax.shard_map(
        shards,
        mesh=mesh,
        in_specs=placed,
        out_specs=(P("col", "row"), P("row", "col"), P("row", "col"), P("col", "row")),
        check_vma=False,
    )
```

```python
import jax
import jax.numpy as jnp
from jax import lax
from jax.experimental import pallas as pl
from jax.experimental.pallas import tpu as pltpu
from jax.sharding import PartitionSpec as P

MESH = pl.DeviceIdType.MESH
F32, BF16 = jnp.float32, jnp.bfloat16
NZ, NY, NX, NH, NC = 4, 2, 4, 2, 2
PLACE = ((0, 0), (0, 1), (1, 0), (3, 0), (1, 1), (3, 1), (2, 0), (2, 1))
UNITS = ((0,), (1,), (2, 3), (4, 5), (6, 7))
SPANS = ((0, 2), (2, 4), (4, 6), (6, 8))
HIDDEN_Y_FIRST = (0, 1, 4)
DELTAS_Y_FIRST = (0, 1, 2, 3, 4)
CUT = 512
IN_FLIGHT = 36
ORDER = (
    0, 13, 12, 40, 52, 53, 80, 90, 16, 20, 32, 14, 15, 17, 100, 81, 72, 60, 54, 82, 55, 130, 56, 91, 57, 92,
    33, 102, 83, 73, 34, 132, 93, 112, 84, 74, 103, 122, 94, 104, 113, 142, 114, 152, 134, 133, 124, 110, 162,
    123, 144, 154, 172, 182, 143, 164, 174, 153, 192, 252, 184, 120, 101, 301, 291, 111, 202, 163, 262, 194,
    254, 131, 140, 121, 150, 264, 212, 303, 173, 183, 203, 141, 151, 160, 293, 222, 161, 193, 253, 213, 170,
    171, 200, 292, 180, 263, 181, 201, 210, 242, 204, 223, 302, 190, 250, 191, 211, 251, 214, 221, 290, 260,
    230, 220, 261, 270, 224, 231, 311, 234, 300, 243, 312, 241, 240, 310, 244, 313, 280,
)


def nn(a, b):
    return lax.dot_general(a, b, (((1,), (0,)), ((), ())), preferred_element_type=F32)


def nt(a, b):
    return lax.dot_general(a, b, (((1,), (1,)), ((), ())), preferred_element_type=F32)


def tn(a, b):
    return lax.dot_general(a, b, (((0,), (0,)), ((), ())), preferred_element_type=F32)


def scratch(dims):
    D, F, R = dims["D"], dims["F"], dims["R"]
    U = NX * NH
    v = pltpu.VMEM
    shapes = {
        "wg": v((D, F), BF16),
        "wu": v((D, F), BF16),
        "wd": v((F, D), BF16),
        "xa": v((2, U, NC, R, D), BF16),
        "hgu": v((3, U * NC * R, F), BF16),
        "ig_o": v((U, R, D), F32),
        "ig_m": v((U, R, D), F32),
        "co_r": v((U, R, D), F32),
        "xs_r": v((U, R, D), F32),
        "h_s": v((R, D), BF16),
        "h_r": v((R, D), BF16),
        "acc_g": v((D, F), F32),
        "acc_u": v((D, F), F32),
        "acc_d": v((F, D), F32),
        "ssem": pltpu.SemaphoreType.DMA((240,)),
        "rsem": pltpu.SemaphoreType.DMA((240,)),
        "lsem": pltpu.SemaphoreType.DMA((5,)),
    }
    for b, units in enumerate(UNITS):
        T = len(units) * NC * R
        O = T // (NZ * NY)
        if b < 4:
            shapes["part", b] = v((3, T, F), F32)
        for name in ("far", "dir", "rel"):
            shapes[name, 0, b] = shapes[name, 1, b] = v((2, 2, O, F), BF16)
        shapes["ry", 0, b] = shapes["ry", 1, b] = v((2, O, F), BF16)
        shapes["sy", 0, b] = shapes["sy", 1, b] = v((NZ * O, F), BF16)
        for name in ("sf", "sd", "sr"):
            shapes[name, 0, b] = shapes[name, 1, b] = v((O, F), BF16)
        shapes["z_own", b] = v((2, O, F), F32)
        shapes["s_own", b] = v((O, F), F32)
    return shapes


def kernel(dims, names, x_hbm, c_hbm, wg_hbm, wu_hbm, wd_hbm, ig_ref, gg_ref, ug_ref, dg_ref, *refs):
    D, F, R = dims["D"], dims["F"], dims["R"]
    s = dict(zip(names, refs))
    row, col = lax.axis_index("row"), lax.axis_index("col")
    yi, zi = row // NZ, row % NZ
    xi, hi, ci = col // (NH * NC), (col // NC) % NH, col % NC
    y_o = 1 - yi

    def zn(k):
        return (zi + k) % NZ

    def at_z(k):
        return (yi * NZ + zn(k), col)

    def at_x(k):
        return (row, ((xi + k) % NX) * (NH * NC) + hi * NC + ci)

    at_y = (y_o * NZ + zi, col)
    at_h = (row, xi * (NH * NC) + (1 - hi) * NC + ci)
    at_c = (row, xi * (NH * NC) + hi * NC + 1 - ci)
    xa, hgu = s["xa"], s["hgu"]
    low, high = pl.ds(0, CUT), pl.ds(CUT, F - CUT)
    ways = ((0, 1), (1, 3))

    def back(u):
        k, h = PLACE[u]
        return PLACE.index((-k % NX, h)), k

    def tokens(b):
        return len(UNITS[b]) * NC * R

    def owned(b):
        return tokens(b) // (NZ * NY)

    def start(b):
        return UNITS[b][0] * NC * R

    def rows(b, y, z, count=1):
        O = owned(b)
        return pl.ds(pl.multiple_of((y * NZ + z) * O, O), O * count)

    def all_rows(b, y, z, count=1):
        O = owned(b)
        return pl.ds(pl.multiple_of(start(b) + (y * NZ + z) * O, O), O * count)

    def part(b):
        return s["part", b if b < 4 else b - 2]

    loads = [
        pltpu.make_async_copy(src, dst, s["lsem"].at[i])
        for i, (src, dst) in enumerate(
            (
                (x_hbm, xa.at[0, 0, 0]),
                (c_hbm, xa.at[1, 0, 0]),
                (wg_hbm, s["wg"]),
                (wu_hbm, s["wu"]),
                (wd_hbm, s["wd"]),
            )
        )
    ]
    for load in loads:
        load.start()

    barrier = pltpu.get_barrier_semaphore()
    peers = [at_c, at_h, at_y, at_z(1), at_z(3), at_x(1), at_x(3), at_x(2)]
    for peer in peers:
        pl.semaphore_signal(barrier, inc=1, device_id=peer, device_id_type=MESH)
    pl.semaphore_wait(barrier, len(peers))

    msgs, leaving = {}, []

    def send(key, src, dst, peer):
        i = len(msgs)
        copy = pltpu.make_async_remote_copy(
            src, dst, s["ssem"].at[i], s["rsem"].at[i], device_id=peer, device_id_type=MESH
        )
        copy.start()
        msgs[key] = copy
        leaving.append(copy)

    def got(*key):
        msgs[key].wait_recv()

    def gather(a):
        def own(b):
            loads[a].wait()
            send(("aC", a, 0), xa.at[a, 0, 0], xa.at[a, 0, 1], at_c)
            send(("ah", a), xa.at[a, 0, 0], xa.at[a, 1, 0], at_h)

        def along(u):
            there, k = back(u)
            src = xa.at[a, PLACE[u][1], 0]
            send(("ax", a, there), src, xa.at[a, there, 0], at_x(k))

        def across(b):
            got("ah", a)
            send(("aC", a, 1), xa.at[a, 1, 0], xa.at[a, 1, 1], at_c)

        def twin(b):
            for u in UNITS[b]:
                got("ax", a, u)
            here = pl.ds(UNITS[b][0], len(UNITS[b]))
            send(("aC", a, b), xa.at[a, here, 0], xa.at[a, here, 1], at_c)

        return [own, along, across, twin]

    def block(a, b):
        return xa[a, UNITS[b][0] : UNITS[b][-1] + 1].reshape(tokens(b), D)

    def send_z(name, b, way, k, dims=()):
        at = dims or (way,)
        send((name, way, b), s[name, 0, b].at[at], s[name, 1, b].at[at], at_z(k))

    def s1g(b):
        got("aC", 0, b)
        if b == 0:
            loads[2].wait()
            loads[3].wait()
        p = part(b)
        x_all = block(0, b)
        p[0] = nn(x_all, s["wg"][...])
        p[1] = nn(x_all, s["wu"][...])
        for half, k in ways:
            for i in range(2):
                s["far", 0, b][half, i] = p[i, rows(b, half, zn(2))].astype(BF16)
            send_z("far", b, half, k)
        for way, k in ways:
            for i in range(2):
                s["dir", 0, b][way, i] = p[i, rows(b, 1 - way, zn(k))].astype(BF16)
            send_z("dir", b, way, k)

    def s1s(b):
        got("aC", 1, b)
        if b == 0:
            loads[4].wait()
        p = part(b)
        p[2] = nt(block(1, b), s["wd"][...])
        s["sy", 0, b][...] = p[2, rows(b, y_o, 0, NZ)].astype(BF16)
        send(("sy", b), s["sy", 0, b], s["sy", 1, b], at_y)

    def s2(b):
        for half, k in ways:
            got("far", half, b)
            for i in range(2):
                total = part(b)[i, rows(b, half, zn(k))] + s["far", 1, b][half, i].astype(F32)
                s["rel", 0, b][half, i] = total.astype(BF16)
            send_z("rel", b, half, k)

    def pair(b, k, cols):
        return part(b)[2, rows(b, yi, zn(k)), cols] + s["sy", 1, b][rows(b, 0, zn(k)), cols].astype(F32)

    every = slice(None)

    def s3(b):
        got("sy", b)
        s["sf", 0, b][...] = pair(b, 2, every).astype(BF16)
        send_z("sf", b, 0, 1, (every, low))
        send_z("sf", b, 1, 3, (every, high))
        s["sd", 0, b][:, high] = pair(b, 1, high).astype(BF16)
        send_z("sd", b, 0, 1, (every, high))
        s["sd", 0, b][:, low] = pair(b, 3, low).astype(BF16)
        send_z("sd", b, 1, 3, (every, low))
        s["s_own", b][...] = pair(b, 0, every)

    def s3b(b):
        for way, k, cols in ((0, 1, low), (1, 3, high)):
            got("sf", way, b)
            s["sr", 0, b][:, cols] = (pair(b, k, cols) + s["sf", 1, b][:, cols].astype(F32)).astype(BF16)
            send_z("sr", b, way, k, (every, cols))

    def s4(b):
        for half in range(2):
            got("dir", 1 - half, b)
            got("rel", half, b)

        def total(i, y):
            here = part(b)[i, rows(b, y, zi)]
            return here + s["rel", 1, b][y, i].astype(F32) + s["dir", 1, b][1 - y, i].astype(F32)

        for i in range(2):
            s["ry", 0, b][i] = total(i, y_o).astype(BF16)
        send(("ry", b), s["ry", 0, b], s["ry", 1, b], at_y)
        for i in range(2):
            s["z_own", b][i] = total(i, yi)

    def s5(b):
        got("ry", b)
        for way in range(2):
            got("sr", way, b)
            got("sd", way, b)
        for j in range(0, owned(b), 16):
            at = slice(j, j + 16)
            gate = s["z_own", b][0, at] + s["ry", 1, b][0, at].astype(F32)
            up = s["z_own", b][1, at] + s["ry", 1, b][1, at].astype(F32)
            slope = s["s_own", b][at] + s["sr", 1, b][at].astype(F32) + s["sd", 1, b][at].astype(F32)
            sig = jax.nn.sigmoid(gate)
            act = gate * sig
            deriv = sig * (1.0 + gate * (1.0 - sig))
            to = pl.ds(pl.multiple_of(start(b) + (yi * NZ + zi) * owned(b) + j, 16), 16)
            hgu[0, to] = (act * up).astype(BF16)
            hgu[1, to] = (slope * up * deriv).astype(BF16)
            hgu[2, to] = (slope * act).astype(BF16)

    def spread(first, count, y_first):
        arrays = pl.ds(first, count)

        def put(name, way, b, at, peer):
            here = hgu.at[(arrays,) + at]
            send((name, way, b, first), here, here, peer)

        def begin(b):
            mine = (all_rows(b, yi, zi),)
            if b in y_first:
                put("cy", 0, b, mine, at_y)
            for way, k in ways:
                put("cz", way, b, mine, at_z(k))

        def second(b):
            if b in y_first:
                got("cy", 0, b, first)
                for way, k in ways:
                    put("cu", way, b, (all_rows(b, y_o, zi),), at_z(k))
            else:
                for way, k, cols in ((0, 1, low), (1, 3, high)):
                    got("cz", way, b, first)
                    put("cf", way, b, (all_rows(b, yi, zn(-k % NZ)), cols), at_z(k))

        def third(b):
            if b in y_first:
                got("cz", 0, b, first)
                put("cf", 0, b, (all_rows(b, yi, zn(3)),), at_z(1))
                got("cz", 1, b, first)
            else:
                got("cf", 0, b, first)
                got("cf", 1, b, first)
                put("cy", 0, b, (all_rows(b, yi, 0, NZ),), at_y)

        def fourth(b):
            got("cu", 1, b, first)
            put("cf", 1, b, (all_rows(b, y_o, zn(1)),), at_z(3))
            got("cu", 0, b, first)

        def last(b):
            if b in y_first:
                got("cf", 0, b, first)
                got("cf", 1, b, first)
            else:
                got("cy", 0, b, first)

        return [begin, second, third, fourth, last]

    def s8(b):
        n = len(UNITS[b])
        here = pl.ds(UNITS[b][0], n)

        def of_core(core):
            at = slice(start(b), start(b) + tokens(b))
            gd = hgu[1, at].reshape(n, NC, R, F)[:, core].reshape(n * R, F)
            ud = hgu[2, at].reshape(n, NC, R, F)[:, core].reshape(n * R, F)
            return (nt(gd, s["wg"][...]) + nt(ud, s["wu"][...])).reshape(n, R, D)

        s["ig_o"][here] = of_core(1)
        send(("co", b), s["ig_o"].at[here], s["co_r"].at[here], at_c)
        s["ig_m"][here] = of_core(0)

    def s10(b):
        got("co", b)
        here = pl.ds(UNITS[b][0], len(UNITS[b]))
        s["ig_m"][here] += s["co_r"][here]
        if b >= 2:
            for u in UNITS[b]:
                there, k = back(u)
                send(("xs", there), s["ig_m"].at[u], s["xs_r"].at[there], at_x(k))

    def gathered(h):
        total = s["ig_m"][h]
        for u, (k, other) in enumerate(PLACE):
            if k and other == h:
                total = total + s["xs_r"][u]
        return total

    def s11(b):
        for u in range(2, len(PLACE)):
            got("xs", u)
        s["h_s"][...] = gathered(1).astype(BF16)
        send(("h",), s["h_s"], s["h_r"], at_h)

    def s12(b):
        mine = gathered(0)
        got("h")
        ig_ref[...] = (mine + s["h_r"][...].astype(F32)).astype(BF16)

    def grad(left, right, acc, out):
        seen = []

        def g(step):
            seen.append(step)
            if len(seen) == 1:
                acc[...] = tn(left(step), right(step))
            elif len(seen) < len(SPANS):
                acc[...] += tn(left(step), right(step))
            else:
                out[...] = (acc[...] + tn(left(step), right(step))).astype(BF16)

        return g

    def activations(a):
        def pick(step):
            first, end = SPANS[step]
            return xa[a, first:end].reshape(-1, D)

        return pick

    def results(a):
        def pick(step):
            first, end = SPANS[step]
            return hgu[a, first * NC * R : end * NC * R]

        return pick

    tasks = [*gather(0), *gather(1), s1g, s1s, s2, s3, s3b, s4, s5]
    tasks += [*spread(1, 2, DELTAS_Y_FIRST), *spread(0, 1, HIDDEN_Y_FIRST), s8, s10, s11, s12]
    tasks.append(grad(activations(0), results(1), s["acc_g"], gg_ref))
    tasks.append(grad(activations(0), results(2), s["acc_u"], ug_ref))
    tasks.append(grad(results(0), activations(1), s["acc_d"], dg_ref))
    for entry in ORDER:
        tasks[entry // 10](entry % 10)
        while len(leaving) > IN_FLIGHT:
            leaving.pop(0).wait_send()

    for copy in leaving:
        copy.wait_send()


def place(*refs):
    n = 4
    moves = [pltpu.make_async_copy(refs[a], refs[n + a], refs[2 * n].at[a]) for a in range(n)]
    for move in moves:
        move.start()
    for move in moves:
        move.wait()


def shards(x, c, wg, wu, wd):
    R, D = x.shape
    F = wg.shape[1]
    dims = {"D": D, "F": F, "R": R}
    shapes = scratch(dims)
    vmem, anywhere = pl.BlockSpec(memory_space=pltpu.VMEM), pl.BlockSpec(memory_space=pl.ANY)
    names = tuple(shapes)

    def body(*refs):
        kernel(dims, names, *refs)

    out_shape = [jax.ShapeDtypeStruct(a.shape, BF16) for a in (x, wg, wu, wd)]
    outs = pl.pallas_call(
        body,
        name="swiglu_block",
        out_shape=[pltpu.VMEM(a.shape, BF16) for a in out_shape],
        in_specs=[anywhere] * 5,
        out_specs=[vmem] * 4,
        scratch_shapes=list(shapes.values()),
        compiler_params=pltpu.CompilerParams(collective_id=0, has_side_effects=True, vmem_limit_bytes=55 * 2**20),
        cost_estimate=pl.CostEstimate(flops=16 * NX * NH * NC * R * D * F, bytes_accessed=6 * D * F, transcendentals=0),
    )(x, c, wg, wu, wd)
    return tuple(
        pl.pallas_call(
            place,
            name="place_outputs",
            out_shape=out_shape,
            in_specs=[vmem] * 4,
            out_specs=[anywhere] * 4,
            scratch_shapes=[pltpu.SemaphoreType.DMA((4,))],
            compiler_params=pltpu.CompilerParams(vmem_limit_bytes=2 * 2**20),
            cost_estimate=pl.CostEstimate(flops=0, bytes_accessed=6 * D * F, transcendentals=0),
        )(*(pltpu.with_memory_space_constraint(out, pltpu.VMEM) for out in outs))
    )


def solution(mesh):
    placed = (P("col", "row"), P("col", "row"), P("row", "col"), P("row", "col"), P("col", "row"))
    return jax.shard_map(
        shards,
        mesh=mesh,
        in_specs=placed,
        out_specs=(P("col", "row"), P("row", "col"), P("row", "col"), P("col", "row")),
        check_vma=False,
    )
```

```python
import jax
import jax.numpy as jnp
from jax import lax
from jax.experimental import pallas as pl
from jax.experimental.pallas import tpu as pltpu
from jax.sharding import PartitionSpec as P

MESH = pl.DeviceIdType.MESH
F32, BF16 = jnp.float32, jnp.bfloat16
NZ, NY, NX, NH, NC = 4, 2, 4, 2, 2
PLACE = ((0, 0), (0, 1), (1, 0), (3, 0), (1, 1), (3, 1), (2, 0), (2, 1))
UNITS = ((0,), (1,), (2, 3), (4, 5), (6, 7))
SPANS = ((0, 2), (2, 4), (4, 6), (6, 8))
HIDDEN_Y_FIRST = (0, 1, 4,)
DELTAS_Y_FIRST = (0, 1, 2, 3, 4,)
CUT = 512
IN_FLIGHT = 36
ORDER = (
    0, 12, 13, 40, 53, 52, 16, 80, 20, 32, 15, 90, 100, 14, 81, 72, 17, 60, 54, 55, 82, 56, 92, 33, 91, 102,
    57, 83, 34, 130, 73, 112, 132, 84, 93, 74, 122, 103, 94, 104, 142, 152, 114, 162, 134, 124, 113, 111, 172,
    133, 182, 144, 154, 123, 164, 110, 192, 101, 252, 174, 143, 121, 184, 153, 120, 291, 202, 131, 262, 194,
    163, 254, 293, 141, 140, 150, 264, 212, 301, 173, 183, 203, 151, 303, 222, 161, 160, 193, 253, 213, 171,
    170, 201, 302, 181, 263, 180, 200, 211, 242, 204, 223, 311, 191, 251, 210, 190, 250, 214, 261, 221, 300,
    220, 231, 260, 270, 230, 292, 224, 234, 290, 241, 243, 312, 240, 310, 244, 313, 280,
)


def nn(a, b):
    return lax.dot_general(a, b, (((1,), (0,)), ((), ())), preferred_element_type=F32)


def nt(a, b):
    return lax.dot_general(a, b, (((1,), (1,)), ((), ())), preferred_element_type=F32)


def tn(a, b):
    return lax.dot_general(a, b, (((0,), (0,)), ((), ())), preferred_element_type=F32)


def scratch(dims):
    D, F, R = dims["D"], dims["F"], dims["R"]
    U = NX * NH
    v = pltpu.VMEM
    shapes = {
        "wg": v((D, F), BF16),
        "wu": v((D, F), BF16),
        "wd": v((F, D), BF16),
        "xa": v((2, U, NC, R, D), BF16),
        "hgu": v((3, U * NC * R, F), BF16),
        "ig_o": v((U, R, D), F32),
        "ig_m": v((U, R, D), F32),
        "co_r": v((U, R, D), F32),
        "xs_r": v((U, R, D), F32),
        "h_s": v((R, D), BF16),
        "h_r": v((R, D), BF16),
        "acc_g": v((D, F), F32),
        "acc_u": v((D, F), F32),
        "acc_d": v((F, D), F32),
        "ssem": pltpu.SemaphoreType.DMA((240,)),
        "rsem": pltpu.SemaphoreType.DMA((240,)),
        "lsem": pltpu.SemaphoreType.DMA((5,)),
    }
    for b, units in enumerate(UNITS):
        T = len(units) * NC * R
        O = T // (NZ * NY)
        if b < 4:
            shapes["part", b] = v((3, T, F), F32)
        for name in ("far", "dir", "rel"):
            shapes[name, 0, b] = shapes[name, 1, b] = v((2, 2, O, F), BF16)
        shapes["ry", 0, b] = shapes["ry", 1, b] = v((2, O, F), BF16)
        shapes["sy", 0, b] = shapes["sy", 1, b] = v((NZ * O, F), BF16)
        for name in ("sf", "sd", "sr"):
            shapes[name, 0, b] = shapes[name, 1, b] = v((O, F), BF16)
        shapes["z_own", b] = v((2, O, F), F32)
        shapes["s_own", b] = v((O, F), F32)
    return shapes


def kernel(dims, names, x_hbm, c_hbm, wg_hbm, wu_hbm, wd_hbm, ig_ref, gg_ref, ug_ref, dg_ref, *refs):
    D, F, R = dims["D"], dims["F"], dims["R"]
    s = dict(zip(names, refs))
    row, col = lax.axis_index("row"), lax.axis_index("col")
    yi, zi = row // NZ, row % NZ
    xi, hi, ci = col // (NH * NC), (col // NC) % NH, col % NC
    y_o = 1 - yi

    def zn(k):
        return (zi + k) % NZ

    def at_z(k):
        return (yi * NZ + zn(k), col)

    def at_x(k):
        return (row, ((xi + k) % NX) * (NH * NC) + hi * NC + ci)

    at_y = (y_o * NZ + zi, col)
    at_h = (row, xi * (NH * NC) + (1 - hi) * NC + ci)
    at_c = (row, xi * (NH * NC) + hi * NC + 1 - ci)
    xa, hgu = s["xa"], s["hgu"]
    low, high = pl.ds(0, CUT), pl.ds(CUT, F - CUT)
    ways = ((0, 1), (1, 3))

    def back(u):
        k, h = PLACE[u]
        return PLACE.index((-k % NX, h)), k

    def tokens(b):
        return len(UNITS[b]) * NC * R

    def owned(b):
        return tokens(b) // (NZ * NY)

    def start(b):
        return UNITS[b][0] * NC * R

    def rows(b, y, z, count=1):
        O = owned(b)
        return pl.ds(pl.multiple_of((y * NZ + z) * O, O), O * count)

    def all_rows(b, y, z, count=1):
        O = owned(b)
        return pl.ds(pl.multiple_of(start(b) + (y * NZ + z) * O, O), O * count)

    def part(b):
        return s["part", b if b < 4 else b - 2]

    loads = [
        pltpu.make_async_copy(src, dst, s["lsem"].at[i])
        for i, (src, dst) in enumerate(
            (
                (x_hbm, xa.at[0, 0, 0]),
                (c_hbm, xa.at[1, 0, 0]),
                (wg_hbm, s["wg"]),
                (wu_hbm, s["wu"]),
                (wd_hbm, s["wd"]),
            )
        )
    ]
    for load in loads:
        load.start()

    barrier = pltpu.get_barrier_semaphore()
    peers = [at_c, at_h, at_y, at_z(1), at_z(3), at_x(1), at_x(3), at_x(2)]
    for peer in peers:
        pl.semaphore_signal(barrier, inc=1, device_id=peer, device_id_type=MESH)
    pl.semaphore_wait(barrier, len(peers))

    msgs, leaving = {}, []

    def send(key, src, dst, peer):
        i = len(msgs)
        copy = pltpu.make_async_remote_copy(
            src, dst, s["ssem"].at[i], s["rsem"].at[i], device_id=peer, device_id_type=MESH
        )
        copy.start()
        msgs[key] = copy
        leaving.append(copy)

    def got(*key):
        msgs[key].wait_recv()

    def gather(a):
        def own(b):
            loads[a].wait()
            send(("aC", a, 0), xa.at[a, 0, 0], xa.at[a, 0, 1], at_c)
            send(("ah", a), xa.at[a, 0, 0], xa.at[a, 1, 0], at_h)

        def along(u):
            there, k = back(u)
            src = xa.at[a, PLACE[u][1], 0]
            send(("ax", a, there), src, xa.at[a, there, 0], at_x(k))

        def across(b):
            got("ah", a)
            send(("aC", a, 1), xa.at[a, 1, 0], xa.at[a, 1, 1], at_c)

        def twin(b):
            for u in UNITS[b]:
                got("ax", a, u)
            here = pl.ds(UNITS[b][0], len(UNITS[b]))
            send(("aC", a, b), xa.at[a, here, 0], xa.at[a, here, 1], at_c)

        return [own, along, across, twin]

    def block(a, b):
        return xa[a, UNITS[b][0] : UNITS[b][-1] + 1].reshape(tokens(b), D)

    def send_z(name, b, way, k, dims=()):
        at = dims or (way,)
        send((name, way, b), s[name, 0, b].at[at], s[name, 1, b].at[at], at_z(k))

    def s1g(b):
        got("aC", 0, b)
        if b == 0:
            loads[2].wait()
            loads[3].wait()
        p = part(b)
        x_all = block(0, b)
        p[0] = nn(x_all, s["wg"][...])
        p[1] = nn(x_all, s["wu"][...])
        for half, k in ways:
            for i in range(2):
                s["far", 0, b][half, i] = p[i, rows(b, half, zn(2))].astype(BF16)
            send_z("far", b, half, k)
        for way, k in ways:
            for i in range(2):
                s["dir", 0, b][way, i] = p[i, rows(b, 1 - way, zn(k))].astype(BF16)
            send_z("dir", b, way, k)

    def s1s(b):
        got("aC", 1, b)
        if b == 0:
            loads[4].wait()
        p = part(b)
        p[2] = nt(block(1, b), s["wd"][...])
        s["sy", 0, b][...] = p[2, rows(b, y_o, 0, NZ)].astype(BF16)
        send(("sy", b), s["sy", 0, b], s["sy", 1, b], at_y)

    def s2(b):
        for half, k in ways:
            got("far", half, b)
            for i in range(2):
                total = part(b)[i, rows(b, half, zn(k))] + s["far", 1, b][half, i].astype(F32)
                s["rel", 0, b][half, i] = total.astype(BF16)
            send_z("rel", b, half, k)

    def pair(b, k, cols):
        return part(b)[2, rows(b, yi, zn(k)), cols] + s["sy", 1, b][rows(b, 0, zn(k)), cols].astype(F32)

    every = slice(None)

    def s3(b):
        got("sy", b)
        s["sf", 0, b][...] = pair(b, 2, every).astype(BF16)
        send_z("sf", b, 0, 1, (every, low))
        send_z("sf", b, 1, 3, (every, high))
        s["sd", 0, b][:, high] = pair(b, 1, high).astype(BF16)
        send_z("sd", b, 0, 1, (every, high))
        s["sd", 0, b][:, low] = pair(b, 3, low).astype(BF16)
        send_z("sd", b, 1, 3, (every, low))
        s["s_own", b][...] = pair(b, 0, every)

    def s3b(b):
        for way, k, cols in ((0, 1, low), (1, 3, high)):
            got("sf", way, b)
            s["sr", 0, b][:, cols] = (pair(b, k, cols) + s["sf", 1, b][:, cols].astype(F32)).astype(BF16)
            send_z("sr", b, way, k, (every, cols))

    def s4(b):
        for half in range(2):
            got("dir", 1 - half, b)
            got("rel", half, b)

        def total(i, y):
            here = part(b)[i, rows(b, y, zi)]
            return here + s["rel", 1, b][y, i].astype(F32) + s["dir", 1, b][1 - y, i].astype(F32)

        for i in range(2):
            s["ry", 0, b][i] = total(i, y_o).astype(BF16)
        send(("ry", b), s["ry", 0, b], s["ry", 1, b], at_y)
        for i in range(2):
            s["z_own", b][i] = total(i, yi)

    def s5(b):
        got("ry", b)
        for way in range(2):
            got("sr", way, b)
            got("sd", way, b)
        for j in range(0, owned(b), 16):
            at = slice(j, j + 16)
            gate = s["z_own", b][0, at] + s["ry", 1, b][0, at].astype(F32)
            up = s["z_own", b][1, at] + s["ry", 1, b][1, at].astype(F32)
            slope = s["s_own", b][at] + s["sr", 1, b][at].astype(F32) + s["sd", 1, b][at].astype(F32)
            sig = jax.nn.sigmoid(gate)
            act = gate * sig
            deriv = sig * (1.0 + gate * (1.0 - sig))
            to = pl.ds(pl.multiple_of(start(b) + (yi * NZ + zi) * owned(b) + j, 16), 16)
            hgu[0, to] = (act * up).astype(BF16)
            hgu[1, to] = (slope * up * deriv).astype(BF16)
            hgu[2, to] = (slope * act).astype(BF16)

    def spread(first, count, y_first):
        arrays = pl.ds(first, count)

        def put(name, way, b, at, peer):
            here = hgu.at[(arrays,) + at]
            send((name, way, b, first), here, here, peer)

        def begin(b):
            mine = (all_rows(b, yi, zi),)
            if b in y_first:
                put("cy", 0, b, mine, at_y)
            for way, k in ways:
                put("cz", way, b, mine, at_z(k))

        def second(b):
            if b in y_first:
                got("cy", 0, b, first)
                for way, k in ways:
                    put("cu", way, b, (all_rows(b, y_o, zi),), at_z(k))
            else:
                for way, k, cols in ((0, 1, low), (1, 3, high)):
                    got("cz", way, b, first)
                    put("cf", way, b, (all_rows(b, yi, zn(-k % NZ)), cols), at_z(k))

        def third(b):
            if b in y_first:
                got("cz", 0, b, first)
                put("cf", 0, b, (all_rows(b, yi, zn(3)),), at_z(1))
                got("cz", 1, b, first)
            else:
                got("cf", 0, b, first)
                got("cf", 1, b, first)
                put("cy", 0, b, (all_rows(b, yi, 0, NZ),), at_y)

        def fourth(b):
            got("cu", 1, b, first)
            put("cf", 1, b, (all_rows(b, y_o, zn(1)),), at_z(3))
            got("cu", 0, b, first)

        def last(b):
            if b in y_first:
                got("cf", 0, b, first)
                got("cf", 1, b, first)
            else:
                got("cy", 0, b, first)

        return [begin, second, third, fourth, last]

    def s8(b):
        n = len(UNITS[b])
        here = pl.ds(UNITS[b][0], n)

        def of_core(core):
            at = slice(start(b), start(b) + tokens(b))
            gd = hgu[1, at].reshape(n, NC, R, F)[:, core].reshape(n * R, F)
            ud = hgu[2, at].reshape(n, NC, R, F)[:, core].reshape(n * R, F)
            return (nt(gd, s["wg"][...]) + nt(ud, s["wu"][...])).reshape(n, R, D)

        s["ig_o"][here] = of_core(1)
        send(("co", b), s["ig_o"].at[here], s["co_r"].at[here], at_c)
        s["ig_m"][here] = of_core(0)

    def s10(b):
        got("co", b)
        here = pl.ds(UNITS[b][0], len(UNITS[b]))
        s["ig_m"][here] += s["co_r"][here]
        if b >= 2:
            for u in UNITS[b]:
                there, k = back(u)
                send(("xs", there), s["ig_m"].at[u], s["xs_r"].at[there], at_x(k))

    def gathered(h):
        total = s["ig_m"][h]
        for u, (k, other) in enumerate(PLACE):
            if k and other == h:
                total = total + s["xs_r"][u]
        return total

    def s11(b):
        for u in range(2, len(PLACE)):
            got("xs", u)
        s["h_s"][...] = gathered(1).astype(BF16)
        send(("h",), s["h_s"], s["h_r"], at_h)

    def s12(b):
        mine = gathered(0)
        got("h")
        ig_ref[...] = (mine + s["h_r"][...].astype(F32)).astype(BF16)

    def grad(left, right, acc, out):
        seen = []

        def g(step):
            seen.append(step)
            if len(seen) == 1:
                acc[...] = tn(left(step), right(step))
            elif len(seen) < len(SPANS):
                acc[...] += tn(left(step), right(step))
            else:
                out[...] = (acc[...] + tn(left(step), right(step))).astype(BF16)

        return g

    def activations(a):
        def pick(step):
            first, end = SPANS[step]
            return xa[a, first:end].reshape(-1, D)

        return pick

    def results(a):
        def pick(step):
            first, end = SPANS[step]
            return hgu[a, first * NC * R : end * NC * R]

        return pick

    tasks = [*gather(0), *gather(1), s1g, s1s, s2, s3, s3b, s4, s5]
    tasks += [*spread(1, 2, DELTAS_Y_FIRST), *spread(0, 1, HIDDEN_Y_FIRST), s8, s10, s11, s12]
    tasks.append(grad(activations(0), results(1), s["acc_g"], gg_ref))
    tasks.append(grad(activations(0), results(2), s["acc_u"], ug_ref))
    tasks.append(grad(results(0), activations(1), s["acc_d"], dg_ref))
    for entry in ORDER:
        tasks[entry // 10](entry % 10)
        while len(leaving) > IN_FLIGHT:
            leaving.pop(0).wait_send()

    for copy in leaving:
        copy.wait_send()


def place(*refs):
    n = 4
    moves = [pltpu.make_async_copy(refs[a], refs[n + a], refs[2 * n].at[a]) for a in range(n)]
    for move in moves:
        move.start()
    for move in moves:
        move.wait()


def shards(x, c, wg, wu, wd):
    R, D = x.shape
    F = wg.shape[1]
    dims = {"D": D, "F": F, "R": R}
    shapes = scratch(dims)
    vmem, anywhere = pl.BlockSpec(memory_space=pltpu.VMEM), pl.BlockSpec(memory_space=pl.ANY)
    names = tuple(shapes)

    def body(*refs):
        kernel(dims, names, *refs)

    out_shape = [jax.ShapeDtypeStruct(a.shape, BF16) for a in (x, wg, wu, wd)]
    outs = pl.pallas_call(
        body,
        name="swiglu_block",
        out_shape=[pltpu.VMEM(a.shape, BF16) for a in out_shape],
        in_specs=[anywhere] * 5,
        out_specs=[vmem] * 4,
        scratch_shapes=list(shapes.values()),
        compiler_params=pltpu.CompilerParams(collective_id=0, has_side_effects=True, vmem_limit_bytes=55 * 2**20),
        cost_estimate=pl.CostEstimate(flops=16 * NX * NH * NC * R * D * F, bytes_accessed=6 * D * F, transcendentals=0),
    )(x, c, wg, wu, wd)
    return tuple(
        pl.pallas_call(
            place,
            name="place_outputs",
            out_shape=out_shape,
            in_specs=[vmem] * 4,
            out_specs=[anywhere] * 4,
            scratch_shapes=[pltpu.SemaphoreType.DMA((4,))],
            compiler_params=pltpu.CompilerParams(vmem_limit_bytes=2 * 2**20),
            cost_estimate=pl.CostEstimate(flops=0, bytes_accessed=6 * D * F, transcendentals=0),
        )(*(pltpu.with_memory_space_constraint(out, pltpu.VMEM) for out in outs))
    )


def solution(mesh):
    placed = (P("col", "row"), P("col", "row"), P("row", "col"), P("row", "col"), P("col", "row"))
    return jax.shard_map(
        shards,
        mesh=mesh,
        in_specs=placed,
        out_specs=(P("col", "row"), P("row", "col"), P("row", "col"), P("col", "row")),
        check_vma=False,
    )
```
